32 devices in a mesh: kpt: 2 (over y), row: 4 (over z), col: 2 (over x), rep: 2 (over core).
Axes of the slice: x: 2, y: 2, z: 4, core: 2. Of those that a mesh axis runs over, the one named last changes fastest.
Arguments:
- hamiltonian: bfloat16 [256, 6, 128, 128], P(('kpt', 'row'), 'rep'), parts along dimension 0, may hold values from -0.21875 to 0.21875
- pattern: int32 [128, 6], P('row', 'rep'), may hold values from 0 to 127, as said below
- vectors: bfloat16 [256, 32768], P('col', ('kpt', 'row')), parts along dimension 1, may hold values from -6 to 6
- spectrum: float32 [4], P('kpt'), parts along dimension 0, may hold values from 0.5 to 1.5
Outputs:
- filtered: bfloat16 [256, 32768], P('col', ('kpt', 'row')), parts along dimension 1
- gram: float32 [512, 256], P(('kpt', 'row'), 'col'), parts along dimension 0
The draws below stay inside these ranges and needn't reach their ends.
There are 2 independent parts, one for each index of `kpt`. The reference program is written for one: setup_inputs(seed, part) draws one part's arguments, and reference() takes and returns one part's arrays. A program takes and returns all parts, laid end to end along the dimension named above; an argument that names none is the same for every part. Nothing has to cross between parts.
Inputs may be any that keep to these rules, and one draw needn't show every extreme that they name: Each block row i names 6 different blocks; pattern[i, 0] = i, pattern[i, 1] = (i - 1) mod 128, pattern[i, 2] = (i + 1) mod 128, and every entry is (i + o) mod 128 with |o| <= 63.
All inputs are finite; a program needn't handle non-finite values.
Results may differ from the reference program's by a relative error of at most 0.0085.
Values may be sent and summed in bfloat16 or wider, within the bound.
A program may use at most 64 MiB of HBM per device.

```python
import jax
import jax.numpy as jnp
from jax import lax

B = 128
K = 256
NNZ = 6
RB_DEV = 32
NB = 128
N = 16384


def draw_pattern(key, part):
    key = jax.random.fold_in(key, 7)
    reach = 2 * RB_DEV - 1
    lower = jnp.arange(-reach, -1, dtype=jnp.int32)
    upper = jnp.arange(2, reach + 1, dtype=jnp.int32)
    offsets = jnp.concatenate([lower, upper])
    many = offsets.shape[0]
    scores = jax.random.randint(key, (NB, many), 0, 1 << 20) * many + jnp.arange(many, dtype=jnp.int32)[None, :]
    order = jnp.argsort(scores, axis=1)
    chosen = offsets[order[:, :NNZ - 3]]
    fixed_part = jnp.broadcast_to(jnp.array([0, -1, 1], dtype=jnp.int32), (NB, 3))
    every = jnp.concatenate([fixed_part, chosen], axis=1)
    rows_all = jnp.arange(NB, dtype=jnp.int32)[:, None]
    return ((rows_all + every) % NB).astype(jnp.int32)


def steps_of(stream_key, dims, split, low, largest):
    def one(dim, shards_of):
        steps = jax.random.uniform(jax.random.fold_in(jax.random.fold_in(stream_key, 6), dim), (shards_of,), jnp.float32, low / len(split), largest / len(split))
        return jnp.repeat(jnp.exp(steps), dims[dim] // shards_of).reshape((-1,) + (1,) * (len(dims) - dim - 1))

    level = one(*split[0])
    for cut in split[1:]:
        level = level * one(*cut)
    return level


def gaussian(own_key, dims, width, most, cuts=(), kind=jnp.bfloat16):
    entries = width * jax.random.normal(own_key, dims, jnp.float32)
    if cuts:
        entries = entries * steps_of(own_key, dims, cuts, -0.22, 0.18)
    return jnp.clip(entries, -most, most).astype(kind)


def setup_inputs(seed: int = 0, part: int = 0) -> dict:
    key_list = jax.random.split(jax.random.key(seed), 5)
    own_keys = jax.random.split(jax.random.fold_in(key_list[4], part), 5)
    hamiltonian = gaussian(own_keys[0], (NB, NNZ, B, B), (NNZ * B) ** -0.5, 0.21875, ((0, 4), (1, 2)))
    pattern = draw_pattern(jax.random.fold_in(key_list[4], 71), part)
    vectors = gaussian(own_keys[2], (K, N), 1.0, 6.0, ((0, 2), (1, 4)))
    spectrum = jnp.clip(jax.random.uniform(own_keys[3], (2,), jnp.float32, 0.5, 1.5), 0.5, 1.5)
    return dict(hamiltonian=hamiltonian, pattern=pattern, vectors=vectors, spectrum=spectrum)


def apply_blocks(hamiltonian, pattern, slab):
    count = slab.shape[0]
    blocks = slab.reshape(count, NB, B)

    def one_row(item):
        stored, columns = item
        picked = jnp.take(blocks, columns.astype(jnp.int32), axis=1).astype(jnp.float32)
        return jnp.einsum("ksc,src->kr", picked, stored.astype(jnp.float32))

    result = lax.map(one_row, (hamiltonian, pattern))
    return jnp.transpose(result, (1, 0, 2)).reshape(count, NB * B)


def reference(hamiltonian, pattern, vectors, spectrum):
    centre = spectrum[0]
    half_width = spectrum[1]
    start = vectors.astype(jnp.float32)
    product = apply_blocks(hamiltonian, pattern, vectors)
    first = (1.0 * (product - centre * start) / half_width).astype(jnp.bfloat16)
    product = apply_blocks(hamiltonian, pattern, first)
    filtered = (2.0 * (product - centre * first.astype(jnp.float32)) / half_width - start).astype(jnp.bfloat16)
    gram = jnp.dot(filtered, filtered.T, preferred_element_type=jnp.float32) / (NB * B)
    return filtered, gram
```

```python
import functools

import jax
import jax.numpy as jnp
from jax import lax
from jax.experimental import pallas as pl
from jax.experimental.pallas import tpu as pltpu
from jax.sharding import PartitionSpec as P

MESH = pl.DeviceIdType.MESH
NT = (((1,), (1,)), ((), ()))
CHUNKS = 2
UNROLL = 4


def kernel(
    R, C, hops, line, h_ref, pat_ref, vec_ref, spec_ref, out_ref, gram_ref,
    hall, pvm, psm, stage, filt, gbuf, part, recv_a, send_b, recv_b, *rest,
):
    wins = rest[: 2 * CHUNKS]
    (z_send, z_recv, h_send, h_recv, p_send, p_recv, loc, o_send, o_recv,
     g_send, g_recv, a_send, a_recv, b_send, b_recv) = rest[2 * CHUNKS:]
    win1, win2 = wins[:CHUNKS], wins[CHUNKS:]
    k, r, c, p = (lax.axis_index(n) for n in ("kpt", "row", "col", "rep"))
    G = 2 * C
    g = c * 2 + p
    nb, half_nnz = h_ref.shape[0], h_ref.shape[1]
    B = h_ref.shape[2]
    V = stage.shape[0]
    vc = V // CHUNKS
    bw = gbuf.shape[1]
    ct = part.shape[3]
    rt = send_b.shape[1]
    other = 1 - p

    local_v = pltpu.make_async_copy(vec_ref.at[pl.ds(pl.multiple_of(p * V, V), V)], stage, loc.at[0])
    local_v.start()
    local_h = pltpu.make_async_copy(h_ref, hall.at[p], loc.at[1])
    local_h.start()
    local_p = pltpu.make_async_copy(pat_ref, psm.at[p], loc.at[2])
    local_p.start()

    barrier = pltpu.get_barrier_semaphore()
    for j in range(1, 2 * R):
        o = lax.rem(r * 2 + p + j, 2 * R)
        pl.semaphore_signal(barrier, inc=1, device_id=(k, o // 2, c, lax.rem(o, 2)), device_id_type=MESH)
    for j in range(1, C):
        o = lax.rem(c + j, C)
        for q in range(2):
            pl.semaphore_signal(barrier, inc=1, device_id=(k, r, o, q), device_id_type=MESH)

    def slot(d):
        return r + d if line else 2 + d

    local_v.wait()
    own = slot(0) * nb

    def block_major(i, _):
        for q in range(CHUNKS):
            win1[q][own + i] = stage[pl.ds(q * vc, vc), pl.ds(pl.multiple_of(i * B, B), B)]
        return 0

    lax.fori_loop(0, nb, block_major, 0)
    pl.semaphore_wait(barrier, 2 * R - 1 + 2 * (C - 1))

    def z_copy(step, q, way, h):
        win = (win1, win2)[step][q]
        sign = -1 if way == 0 else 1
        src = slot(sign * h)
        dst = src if line else slot(sign * (h + 1))
        target = r + 1 if way == 0 else r - 1
        target = lax.rem(target + R, R)
        return pltpu.make_async_remote_copy(
            src_ref=win.at[pl.ds(src * nb, nb)],
            dst_ref=win.at[pl.ds(dst * nb, nb)],
            send_sem=z_send.at[step, q, way, h],
            recv_sem=z_recv.at[step, q, way, h],
            device_id=(k, target, c, p),
            device_id_type=MESH,
        )

    def z_arrival(step, q, way, h):
        win = (win1, win2)[step][q]
        sign = -1 if way == 0 else 1
        dst = slot(sign * (h + 1))
        target = lax.rem((r - 1 if way == 0 else r + 1) + R, R)
        return pltpu.make_async_remote_copy(
            src_ref=win.at[pl.ds(dst * nb, nb)],
            dst_ref=win.at[pl.ds(dst * nb, nb)],
            send_sem=z_send.at[step, q, way, h],
            recv_sem=z_recv.at[step, q, way, h],
            device_id=(k, target, c, p),
            device_id_type=MESH,
        )

    def when(cond, fn):
        if line:
            pl.when(cond)(fn)
        else:
            fn()

    def sends(way, h):
        if way == 0:
            return jnp.logical_and(r + 1 < R, r - h >= 0)
        return jnp.logical_and(r - 1 >= 0, r + h < R)

    def receives(way, h):
        return r - 1 - h >= 0 if way == 0 else r + 1 + h < R

    def z_start(step, q, h):
        for way in range(2):
            when(sends(way, h), lambda way=way: z_copy(step, q, way, h).start())

    def z_wait(step, q, h):
        for way in range(2):
            when(receives(way, h), lambda way=way: z_arrival(step, q, way, h).wait_recv())

    def z_forward(step, q, h):
        for way in range(2):
            when(receives(way, h - 1), lambda way=way: z_arrival(step, q, way, h - 1).wait_recv())
            when(sends(way, h), lambda way=way: z_copy(step, q, way, h).start())

    partner = (k, r, c, other)
    for q in range(CHUNKS):
        z_start(0, q, 0)
    send_p = pltpu.make_async_remote_copy(pat_ref, pvm, p_send, p_recv, device_id=partner, device_id_type=MESH)
    send_p.start()
    send_h = pltpu.make_async_remote_copy(h_ref, hall.at[p], h_send, h_recv, device_id=partner, device_id_type=MESH)
    send_h.start()
    arrive_h = pltpu.make_async_remote_copy(h_ref, hall.at[other], h_send, h_recv, device_id=partner, device_id_type=MESH)
    send_p.wait_recv()
    other_p = pltpu.make_async_copy(pvm, psm.at[other], loc.at[3])
    other_p.start()

    for h in range(1, hops):
        for q in range(CHUNKS):
            z_forward(0, q, h)

    local_h.wait()
    local_p.wait()
    other_p.wait()
    arrive_h.wait_recv()

    centre = spec_ref[0]
    inverse = 1.0 / jnp.full((vc, B), spec_ref[1], jnp.float32)
    total = nb * R

    def index(half, i, s):
        named = psm[half, i, s]
        if line:
            return named
        return lax.rem(named - (r - 2) * nb + total, total)

    def product(win, i):
        sums = None
        for half in range(2):
            for s in range(half_nnz):
                term = lax.dot_general(
                    win[index(half, i, s)], hall[half, i, s], NT, preferred_element_type=jnp.float32
                )
                sums = term if sums is None else sums + term
        return sums

    for q in range(CHUNKS):
        z_wait(0, q, hops - 1)

        def first_row(i, _, q=q):
            start = win1[q][own + i].astype(jnp.float32)
            win2[q][own + i] = ((product(win1[q], i) - centre * start) * inverse).astype(jnp.bfloat16)
            return 0

        lax.fori_loop(0, nb, first_row, 0, unroll=UNROLL)
        z_start(1, q, 0)

    for h in range(1, hops):
        for q in range(CHUNKS):
            z_forward(1, q, h)

    def group(j):
        o = lax.rem(g + j, G)
        return o, (k, r, o // 2, lax.rem(o, 2))

    def vec_row(gi, q):
        return pl.ds(pl.multiple_of(gi * V + q * vc, vc), vc)

    tail = []
    for q in range(CHUNKS):
        z_wait(1, q, hops - 1)

        def filtered_row(i, _, q=q):
            first = win2[q][own + i].astype(jnp.float32)
            start = win1[q][own + i].astype(jnp.float32)
            value = 2.0 * ((product(win2[q], i) - centre * first) * inverse) - start
            filt[pl.ds(q * vc, vc), pl.ds(pl.multiple_of(i * B, B), B)] = value.astype(jnp.bfloat16)
            return 0

        lax.fori_loop(0, nb, filtered_row, 0, unroll=UNROLL)
        for j in range(1, G):
            o, device = group(j)
            copy = pltpu.make_async_remote_copy(
                filt.at[pl.ds(q * vc, vc), pl.ds(pl.multiple_of(o * bw, bw), bw)],
                gbuf.at[vec_row(g, q)],
                g_send.at[q, j], g_recv.at[q, j], device_id=device, device_id_type=MESH,
            )
            copy.start()
            tail.append(copy)
        gbuf[vec_row(g, q), :] = filt[pl.ds(q * vc, vc), pl.ds(pl.multiple_of(g * bw, bw), bw)]
        rows = pl.ds(pl.multiple_of(p * V + q * vc, vc), vc)
        keep = pltpu.make_async_copy(filt.at[pl.ds(q * vc, vc)], out_ref.at[rows], loc.at[4 + q])
        keep.start()
        copy = pltpu.make_async_remote_copy(
            filt.at[pl.ds(q * vc, vc)], out_ref.at[rows], o_send.at[q], o_recv.at[q],
            device_id=partner, device_id_type=MESH,
        )
        copy.start()
        tail.append(copy)

    for q in range(CHUNKS):
        for j in range(1, G):
            source = lax.rem(g - j + G, G)
            pltpu.make_async_remote_copy(
                gbuf.at[vec_row(source, q)], gbuf.at[vec_row(source, q)],
                g_send.at[q, j], g_recv.at[q, j], device_id=group(j)[1], device_id_type=MESH,
            ).wait_recv()

    everything = gbuf[...]
    for cc in range(C):
        tile = lax.dot_general(
            everything, gbuf[pl.ds(cc * ct, ct), :], NT, preferred_element_type=jnp.float32
        ).astype(jnp.bfloat16)
        part[cc, 0] = tile[: rt * R // 2]
        part[cc, 1] = tile[rt * R // 2:]
    for j in range(1, G):
        o, device = group(j)
        copy = pltpu.make_async_remote_copy(
            part.at[o // 2, lax.rem(o, 2)], recv_a.at[g], a_send.at[j], a_recv.at[j],
            device_id=device, device_id_type=MESH,
        )
        copy.start()
        tail.append(copy)
    recv_a[g] = part[c, p]
    for j in range(1, G):
        source = lax.rem(g - j + G, G)
        pltpu.make_async_remote_copy(
            recv_a.at[source], recv_a.at[source], a_send.at[j], a_recv.at[j],
            device_id=group(j)[1], device_id_type=MESH,
        ).wait_recv()
    summed = recv_a[0].astype(jnp.float32)
    for j in range(1, G):
        summed = summed + recv_a[j].astype(jnp.float32)
    for j in range(R // 2):
        send_b[j] = summed[j * rt:(j + 1) * rt].astype(send_b.dtype)

    def b_copy(j, q):
        return pltpu.make_async_remote_copy(
            send_b.at[j], recv_b.at[r], b_send.at[j, q], b_recv.at[r],
            device_id=(k, p * (R // 2) + j, c, q), device_id_type=MESH,
        )

    def b_elsewhere(j, q):
        return jnp.logical_or(r != p * (R // 2) + j, p != q)

    for j in range(R // 2):
        for q in range(2):
            pl.when(b_elsewhere(j, q))(lambda j=j, q=q: b_copy(j, q).start())
        pl.when(r == p * (R // 2) + j)(lambda j=j: recv_b.__setitem__(r, send_b[j]))
    mine = r // (R // 2)
    for source in range(R):
        arrive = pltpu.make_async_remote_copy(
            recv_b.at[source], recv_b.at[source], b_send.at[0, 0], b_recv.at[source],
            device_id=(k, source, c, mine), device_id_type=MESH,
        )
        pl.when(jnp.logical_or(r != source, p != mine))(lambda arrive=arrive: arrive.wait_recv())
    gram = recv_b[0].astype(jnp.float32)
    for source in range(1, R):
        gram = gram + recv_b[source].astype(jnp.float32)
    gram_ref[...] = gram * (1.0 / (total * B))

    for step in range(2):
        for q in range(CHUNKS):
            for h in range(hops):
                for way in range(2):
                    when(sends(way, h), lambda a=(step, q, way, h): z_copy(*a).wait_send())
    send_p.wait_send()
    send_h.wait_send()
    for copy in tail:
        copy.wait_send()
    for j in range(R // 2):
        for q in range(2):
            pl.when(b_elsewhere(j, q))(lambda j=j, q=q: b_copy(j, q).wait_send())
    for q in range(CHUNKS):
        rows = pl.ds(pl.multiple_of(p * V + q * vc, vc), vc)
        pltpu.make_async_copy(filt.at[pl.ds(q * vc, vc)], out_ref.at[rows], loc.at[4 + q]).wait()
        theirs = pl.ds(pl.multiple_of(other * V + q * vc, vc), vc)
        pltpu.make_async_remote_copy(
            filt.at[pl.ds(q * vc, vc)], out_ref.at[theirs], o_send.at[q], o_recv.at[q],
            device_id=partner, device_id_type=MESH,
        ).wait_recv()


def on_device(R, C, hamiltonian, pattern, vectors, spectrum):
    nb, half_nnz, B, _ = hamiltonian.shape
    per_dev, local_rows = vectors.shape
    line = R <= 4
    hops = R - 1 if line else 2
    slots = R if line else 5
    V = per_dev // 2
    vc = V // CHUNKS
    G = 2 * C
    K = per_dev * C
    bw = local_rows // G
    rt, ct = K // R, per_dev
    b_type = jnp.bfloat16 if rt % 16 == 0 else jnp.float32
    bf16 = jnp.bfloat16
    dma = pltpu.SemaphoreType.DMA
    return pl.pallas_call(
        functools.partial(kernel, R, C, hops, line),
        out_shape=(
            jax.ShapeDtypeStruct((per_dev, local_rows), bf16),
            jax.ShapeDtypeStruct((rt, ct), jnp.float32),
        ),
        in_specs=[
            pl.BlockSpec(memory_space=pl.ANY),
            pl.BlockSpec(memory_space=pl.ANY),
            pl.BlockSpec(memory_space=pl.ANY),
            pl.BlockSpec(memory_space=pltpu.SMEM),
        ],
        out_specs=(pl.BlockSpec(memory_space=pl.ANY), pl.BlockSpec(memory_space=pltpu.VMEM)),
        scratch_shapes=[
            pltpu.VMEM((2, nb, half_nnz, B, B), bf16),
            pltpu.VMEM((nb, half_nnz), jnp.int32),
            pltpu.SMEM((2, nb, half_nnz), jnp.int32),
            pltpu.VMEM((V, local_rows), bf16),
            pltpu.VMEM((V, local_rows), bf16),
            pltpu.VMEM((K, bw), bf16),
            pltpu.VMEM((C, 2, K // 2, ct), bf16),
            pltpu.VMEM((G, K // 2, ct), bf16),
            pltpu.VMEM((R // 2, rt, ct), b_type),
            pltpu.VMEM((R, rt, ct), b_type),
        ]
        + [pltpu.VMEM((slots * nb, vc, B), bf16)] * (2 * CHUNKS)
        + [
            dma((2, CHUNKS, 2, hops)), dma((2, CHUNKS, 2, hops)),
            dma, dma, dma, dma, dma((4 + CHUNKS,)),
            dma((CHUNKS,)), dma((CHUNKS,)),
            dma((CHUNKS, G)), dma((CHUNKS, G)),
            dma((G,)), dma((G,)),
            dma((R // 2, 2)), dma((R,)),
        ],
        compiler_params=pltpu.CompilerParams(
            collective_id=0, has_side_effects=True, vmem_limit_bytes=40 * 1024 * 1024
        ),
    )(hamiltonian, pattern, vectors, spectrum)


def solution(mesh):
    in_specs = (
        P(("kpt", "row"), "rep", None, None),
        P("row", "rep"),
        P("col", ("kpt", "row")),
        P("kpt"),
    )
    out_specs = (P("col", ("kpt", "row")), P(("kpt", "row"), "col"))
    return jax.shard_map(
        functools.partial(on_device, mesh.shape["row"], mesh.shape["col"]),
        mesh=mesh, in_specs=in_specs, out_specs=out_specs, check_vma=False,
    )
```

```python
import functools

import jax
import jax.numpy as jnp
from jax import lax
from jax.experimental import pallas as pl
from jax.experimental.pallas import tpu as pltpu
from jax.sharding import PartitionSpec as P

MESH = pl.DeviceIdType.MESH
NT = (((1,), (1,)), ((), ()))
NN = (((1,), (0,)), ((), ()))
UNROLL = 8


def kernel(
    R, C, hops, line, chunks, h_ref, pat_ref, vec_ref, spec_ref, out_ref, gram_ref,
    hall, pvm, psm, stage, filt, gbuf, part, recv_a, send_b, recv_b, *rest,
):
    wins = rest[: 2 * chunks]
    (z_send, z_recv, h_send, h_recv, p_send, p_recv, loc, o_send, o_recv,
     g_send, g_recv, a_send, a_recv, b_send, b_recv) = rest[2 * chunks:2 * chunks + 15]
    extra = rest[2 * chunks + 15:]
    win1, win2 = wins[:chunks], wins[chunks:]
    ends = bool(extra)
    if ends:
        hx, pxv, pxs = extra[:3]
        s_out, s_in = extra[3:3 + chunks], extra[3 + chunks:3 + 2 * chunks]
        x_send, x_recv, y_send, y_recv, px_send, px_recv, s_send, s_recv, e_send, e_recv = extra[3 + 2 * chunks:]
    k, r, c, p = (lax.axis_index(n) for n in ("kpt", "row", "col", "rep"))
    G = 2 * C
    g = c * 2 + p
    nb, half_nnz = h_ref.shape[0], h_ref.shape[1]
    B = h_ref.shape[2]
    V = stage.shape[0]
    vc = V // chunks
    bw = gbuf.shape[1]
    ct = part.shape[3]
    rt = send_b.shape[1]
    other = 1 - p

    local_v = pltpu.make_async_copy(vec_ref.at[pl.ds(pl.multiple_of(p * V, V), V)], stage, loc.at[0])
    local_v.start()
    local_h = pltpu.make_async_copy(h_ref, hall.at[p], loc.at[1])
    local_h.start()
    local_p = pltpu.make_async_copy(pat_ref, psm.at[p], loc.at[2])
    local_p.start()

    barrier = pltpu.get_barrier_semaphore()
    for j in range(1, 2 * R):
        o = lax.rem(r * 2 + p + j, 2 * R)
        pl.semaphore_signal(barrier, inc=1, device_id=(k, o // 2, c, lax.rem(o, 2)), device_id_type=MESH)
    for j in range(1, C):
        o = lax.rem(c + j, C)
        for q in range(2):
            pl.semaphore_signal(barrier, inc=1, device_id=(k, r, o, q), device_id_type=MESH)

    def slot(d):
        return r + d if line else 2 + d

    local_v.wait()
    own = slot(0) * nb

    def block_major(i, _):
        for q in range(chunks):
            win1[q][own + i] = stage[pl.ds(q * vc, vc), pl.ds(pl.multiple_of(i * B, B), B)]
        return 0

    lax.fori_loop(0, nb, block_major, 0)
    pl.semaphore_wait(barrier, 2 * R - 1 + 2 * (C - 1))

    def z_copy(step, q, way, h):
        win = (win1, win2)[step][q]
        sign = -1 if way == 0 else 1
        src = slot(sign * h)
        dst = src if line else slot(sign * (h + 1))
        target = r + 1 if way == 0 else r - 1
        target = lax.rem(target + R, R)
        return pltpu.make_async_remote_copy(
            src_ref=win.at[pl.ds(src * nb, nb)],
            dst_ref=win.at[pl.ds(dst * nb, nb)],
            send_sem=z_send.at[step, q, way, h],
            recv_sem=z_recv.at[step, q, way, h],
            device_id=(k, target, c, p),
            device_id_type=MESH,
        )

    def z_arrival(step, q, way, h):
        win = (win1, win2)[step][q]
        sign = -1 if way == 0 else 1
        dst = slot(sign * (h + 1))
        target = lax.rem((r - 1 if way == 0 else r + 1) + R, R)
        return pltpu.make_async_remote_copy(
            src_ref=win.at[pl.ds(dst * nb, nb)],
            dst_ref=win.at[pl.ds(dst * nb, nb)],
            send_sem=z_send.at[step, q, way, h],
            recv_sem=z_recv.at[step, q, way, h],
            device_id=(k, target, c, p),
            device_id_type=MESH,
        )

    if ends:
        outer = jnp.logical_or(r == 0, r == R - 1)
        inner = jnp.logical_not(outer)
        low = r < R // 2
        end = jnp.where(low, 0, R - 1)
        mate = jnp.where(low, 1 - r, 2 * R - 3 - r)
        zero_block = nb * R
        edge_near = jnp.where(low, nb, (R - 1) * nb - 1)
        edge_far = jnp.where(low, nb * R - 1, 0)

    def when(cond, fn):
        if line:
            pl.when(cond)(fn)
        else:
            fn()

    def sends(step, way, h):
        short = 1 if ends and step == 1 else 0
        if way == 0:
            return jnp.logical_and(r + 1 < R - short, r - h >= 0)
        return jnp.logical_and(r - 1 >= short, r + h < R)

    def receives(step, way, h):
        short = 1 if ends and step == 1 else 0
        if way == 0:
            return jnp.logical_and(r < R - short, r - 1 - h >= 0)
        return jnp.logical_and(r >= short, r + 1 + h < R)

    def z_start(step, q, h):
        for way in range(2):
            when(sends(step, way, h), lambda way=way: z_copy(step, q, way, h).start())

    def z_wait(step, q, h):
        for way in range(2):
            when(receives(step, way, h), lambda way=way: z_arrival(step, q, way, h).wait_recv())

    def z_forward(step, q, h):
        for way in range(2):
            when(receives(step, way, h - 1), lambda way=way: z_arrival(step, q, way, h - 1).wait_recv())
            when(sends(step, way, h), lambda way=way: z_copy(step, q, way, h).start())

    partner = (k, r, c, other)
    for q in range(chunks):
        z_start(0, q, 0)
    send_p = pltpu.make_async_remote_copy(pat_ref, pvm, p_send, p_recv, device_id=partner, device_id_type=MESH)
    send_p.start()
    send_h = pltpu.make_async_remote_copy(h_ref, hall.at[p], h_send, h_recv, device_id=partner, device_id_type=MESH)
    send_h.start()
    arrive_h = pltpu.make_async_remote_copy(h_ref, hall.at[other], h_send, h_recv, device_id=partner, device_id_type=MESH)
    if ends:
        piece = nb // 2

        def x_copy(j):
            part_rows = pl.ds(j * piece, piece)
            return pltpu.make_async_remote_copy(
                h_ref.at[part_rows], hx.at[part_rows], x_send.at[j], x_recv.at[j],
                device_id=(k, mate, c, p), device_id_type=MESH,
            )

        def y_copy(j):
            part_rows = pl.ds(j * piece, piece)
            return pltpu.make_async_remote_copy(
                hx.at[part_rows], hx.at[part_rows], y_send.at[j], y_recv.at[j],
                device_id=partner, device_id_type=MESH,
            )

        def px_copy(q):
            return pltpu.make_async_remote_copy(
                pat_ref, pxv, px_send.at[q], px_recv, device_id=(k, mate, c, q), device_id_type=MESH,
            )

        from_end = jnp.logical_and(outer, p == 1)
        relay = jnp.logical_and(inner, p == 1)
        relayed = jnp.logical_and(inner, p == 0)

        @pl.when(from_end)
        def _():
            for q in range(2):
                px_copy(q).start()

        for q in range(chunks):
            win2[q][zero_block] = jnp.zeros((vc, B), jnp.bfloat16)

    send_p.wait_recv()
    other_p = pltpu.make_async_copy(pvm, psm.at[other], loc.at[3])
    other_p.start()

    for h in range(1, hops):
        for q in range(chunks):
            z_forward(0, q, h)

    local_h.wait()
    local_p.wait()
    other_p.wait()
    arrive_h.wait_recv()

    centre = spec_ref[0]
    inverse = 1.0 / jnp.full((vc, B), spec_ref[1], jnp.float32)
    total = nb * R

    def index(half, i, s):
        named = psm[half, s, i]
        if line:
            return named
        return lax.rem(named - (r - 2) * nb + total, total)

    def turn(i, _):
        for half in range(2):
            for s in range(half_nnz):
                hall[half, i, s] = hall[half, i, s].T
        return 0

    lax.fori_loop(0, nb, turn, 0, unroll=2)

    if ends:
        @pl.when(from_end)
        def _():
            for j in range(2):
                x_copy(j).start()

    def product(win, i, held_back=False):
        def place(half, s):
            named = index(half, i, s)
            if held_back and half == 1:
                away = jnp.logical_and(outer, named // nb != r)
                named = jnp.where(away, zero_block, named)
            return named

        picked = [win[place(half, s)] for half in range(2) for s in range(half_nnz)]
        stored = [hall[half, i].reshape(half_nnz * B, B) for half in range(2)]
        return jnp.dot(
            jnp.concatenate(picked, axis=1), jnp.concatenate(stored, axis=0),
            preferred_element_type=jnp.float32,
        )

    if ends:
        @pl.when(inner)
        def _():
            def clear(i, _):
                for q in range(chunks):
                    s_in[q][i] = jnp.zeros((vc, B), jnp.bfloat16)
                return 0

            lax.fori_loop(0, nb, clear, 0)

    for q in range(chunks):
        z_wait(0, q, hops - 1)

        def first_row(i, _, q=q):
            start = win1[q][own + i].astype(jnp.float32)
            win2[q][own + i] = ((product(win1[q], i) - centre * start) * inverse).astype(jnp.bfloat16)
            return 0

        lax.fori_loop(0, nb, first_row, 0, unroll=UNROLL)
        z_start(1, q, 0)

    hops2 = hops - 1 if ends else hops
    for h in range(1, hops2):
        for q in range(chunks):
            z_forward(1, q, h)

    if ends:
        @pl.when(inner)
        def _():
            px_copy(0).wait_recv()
            names = pltpu.make_async_copy(pxv, pxs, loc.at[4 + chunks])
            names.start()
            names.wait()

        @pl.when(relay)
        def _():
            for j in range(2):
                x_copy(j).wait_recv()
                y_copy(j).start()
            for j in range(2):
                y_copy(j).wait_send()

        @pl.when(relayed)
        def _():
            for j in range(2):
                y_copy(j).wait_recv()

        @pl.when(inner)
        def _():
            def turn_x(i, _):
                for s in range(half_nnz):
                    hx[i, s] = hx[i, s].T
                return 0

            lax.fori_loop(0, nb, turn_x, 0, unroll=2)

        def s_copy(q):
            return pltpu.make_async_remote_copy(
                s_out[q], s_in[q], s_send.at[q], s_recv.at[q],
                device_id=(k, mate, c, p), device_id_type=MESH,
            )

        def e_copy(q, which):
            block = pl.ds((edge_near, edge_far)[which], 1)
            return pltpu.make_async_remote_copy(
                win2[q].at[block], win2[q].at[block], e_send.at[q, which], e_recv.at[q, which],
                device_id=(k, mate, c, p), device_id_type=MESH,
            )

    def group(j):
        o = lax.rem(g + j, G)
        return o, (k, r, o // 2, lax.rem(o, 2))

    def vec_row(gi, q):
        return pl.ds(pl.multiple_of(gi * V + q * vc, vc), vc)

    tail = []
    for q in range(chunks):
        z_wait(1, q, hops2 - 1)
        if ends:
            @pl.when(inner)
            def _(q=q):
                for which in range(2):
                    e_copy(q, which).start()

                def end_row(i, _):
                    picked = []
                    for s in range(half_nnz):
                        named = pxs[s, i]
                        picked.append(win2[q][jnp.where(named // nb == end, zero_block, named)])
                    s_out[q][i] = jnp.dot(
                        jnp.concatenate(picked, axis=1), hx[i].reshape(half_nnz * B, B),
                        preferred_element_type=jnp.float32,
                    ).astype(jnp.bfloat16)
                    return 0

                lax.fori_loop(0, nb, end_row, 0, unroll=UNROLL)
                s_copy(q).start()

            @pl.when(outer)
            def _(q=q):
                for which in range(2):
                    e_copy(q, which).wait_recv()
                s_copy(q).wait_recv()

        def filtered_row(i, _, q=q):
            first = win2[q][own + i].astype(jnp.float32)
            start = win1[q][own + i].astype(jnp.float32)
            sums = product(win2[q], i, ends)
            if ends:
                sums = sums + s_in[q][i].astype(jnp.float32)
            value = 2.0 * ((sums - centre * first) * inverse) - start
            filt[pl.ds(q * vc, vc), pl.ds(pl.multiple_of(i * B, B), B)] = value.astype(jnp.bfloat16)
            return 0

        lax.fori_loop(0, nb, filtered_row, 0, unroll=UNROLL)
        for j in range(1, G):
            o, device = group(j)
            copy = pltpu.make_async_remote_copy(
                filt.at[pl.ds(q * vc, vc), pl.ds(pl.multiple_of(o * bw, bw), bw)],
                gbuf.at[vec_row(g, q)],
                g_send.at[q, j], g_recv.at[q, j], device_id=device, device_id_type=MESH,
            )
            copy.start()
            tail.append(copy)
        gbuf[vec_row(g, q), :] = filt[pl.ds(q * vc, vc), pl.ds(pl.multiple_of(g * bw, bw), bw)]
        rows = pl.ds(pl.multiple_of(p * V + q * vc, vc), vc)
        keep = pltpu.make_async_copy(filt.at[pl.ds(q * vc, vc)], out_ref.at[rows], loc.at[4 + q])
        keep.start()
        copy = pltpu.make_async_remote_copy(
            filt.at[pl.ds(q * vc, vc)], out_ref.at[rows], o_send.at[q], o_recv.at[q],
            device_id=partner, device_id_type=MESH,
        )
        copy.start()
        tail.append(copy)

    for q in range(chunks):
        for j in range(1, G):
            source = lax.rem(g - j + G, G)
            pltpu.make_async_remote_copy(
                gbuf.at[vec_row(source, q)], gbuf.at[vec_row(source, q)],
                g_send.at[q, j], g_recv.at[q, j], device_id=group(j)[1], device_id_type=MESH,
            ).wait_recv()

    everything = gbuf[...]
    for cc in range(C):
        tile = lax.dot_general(
            everything, gbuf[pl.ds(cc * ct, ct), :], NT, preferred_element_type=jnp.float32
        ).astype(jnp.bfloat16)
        part[cc, 0] = tile[: rt * R // 2]
        part[cc, 1] = tile[rt * R // 2:]
    for j in range(1, G):
        o, device = group(j)
        copy = pltpu.make_async_remote_copy(
            part.at[o // 2, lax.rem(o, 2)], recv_a.at[g], a_send.at[j], a_recv.at[j],
            device_id=device, device_id_type=MESH,
        )
        copy.start()
        tail.append(copy)
    recv_a[g] = part[c, p]
    for j in range(1, G):
        source = lax.rem(g - j + G, G)
        pltpu.make_async_remote_copy(
            recv_a.at[source], recv_a.at[source], a_send.at[j], a_recv.at[j],
            device_id=group(j)[1], device_id_type=MESH,
        ).wait_recv()
    summed = recv_a[0].astype(jnp.float32)
    for j in range(1, G):
        summed = summed + recv_a[j].astype(jnp.float32)
    for j in range(R // 2):
        send_b[j] = summed[j * rt:(j + 1) * rt].astype(send_b.dtype)

    def b_copy(j, q):
        return pltpu.make_async_remote_copy(
            send_b.at[j], recv_b.at[r], b_send.at[j, q], b_recv.at[r],
            device_id=(k, p * (R // 2) + j, c, q), device_id_type=MESH,
        )

    def b_elsewhere(j, q):
        return jnp.logical_or(r != p * (R // 2) + j, p != q)

    for j in range(R // 2):
        for q in range(2):
            pl.when(b_elsewhere(j, q))(lambda j=j, q=q: b_copy(j, q).start())
        pl.when(r == p * (R // 2) + j)(lambda j=j: recv_b.__setitem__(r, send_b[j]))
    mine = r // (R // 2)
    for source in range(R):
        arrive = pltpu.make_async_remote_copy(
            recv_b.at[source], recv_b.at[source], b_send.at[0, 0], b_recv.at[source],
            device_id=(k, source, c, mine), device_id_type=MESH,
        )
        pl.when(jnp.logical_or(r != source, p != mine))(lambda arrive=arrive: arrive.wait_recv())
    gram = recv_b[0].astype(jnp.float32)
    for source in range(1, R):
        gram = gram + recv_b[source].astype(jnp.float32)
    gram_ref[...] = gram * (1.0 / (total * B))

    for step in range(2):
        for q in range(chunks):
            for h in range(hops):
                for way in range(2):
                    when(sends(step, way, h), lambda a=(step, q, way, h): z_copy(*a).wait_send())
    if ends:
        @pl.when(from_end)
        def _():
            for j in range(2):
                px_copy(j).wait_send()
                x_copy(j).wait_send()

        @pl.when(inner)
        def _():
            for q in range(chunks):
                s_copy(q).wait_send()
                for which in range(2):
                    e_copy(q, which).wait_send()
    send_p.wait_send()
    send_h.wait_send()
    for copy in tail:
        copy.wait_send()
    for j in range(R // 2):
        for q in range(2):
            pl.when(b_elsewhere(j, q))(lambda j=j, q=q: b_copy(j, q).wait_send())
    for q in range(chunks):
        rows = pl.ds(pl.multiple_of(p * V + q * vc, vc), vc)
        pltpu.make_async_copy(filt.at[pl.ds(q * vc, vc)], out_ref.at[rows], loc.at[4 + q]).wait()
        theirs = pl.ds(pl.multiple_of(other * V + q * vc, vc), vc)
        pltpu.make_async_remote_copy(
            filt.at[pl.ds(q * vc, vc)], out_ref.at[theirs], o_send.at[q], o_recv.at[q],
            device_id=partner, device_id_type=MESH,
        ).wait_recv()


def on_device(R, C, hamiltonian, pattern, vectors, spectrum):
    nb, half_nnz, B, _ = hamiltonian.shape
    per_dev, local_rows = vectors.shape
    line = R <= 4
    hops = R - 1 if line else 2
    slots = R if line else 5
    V = per_dev // 2
    chunks = 4 if V % 64 == 0 else max(V // 16, 1)
    vc = V // chunks
    G = 2 * C
    K = per_dev * C
    bw = local_rows // G
    rt, ct = K // R, per_dev
    b_type = jnp.bfloat16 if rt % 16 == 0 else jnp.float32
    bf16 = jnp.bfloat16
    dma = pltpu.SemaphoreType.DMA
    end_scratch = []
    if R == 4:
        end_scratch = [
            pltpu.VMEM((nb, half_nnz, B, B), bf16),
            pltpu.VMEM((half_nnz, nb), jnp.int32),
            pltpu.SMEM((half_nnz, nb), jnp.int32),
        ] + [pltpu.VMEM((nb, vc, B), bf16)] * (2 * chunks) + [
            dma((2,)), dma((2,)), dma((2,)), dma((2,)), dma((2,)), dma,
            dma((chunks,)), dma((chunks,)), dma((chunks, 2)), dma((chunks, 2)),
        ]
    return pl.pallas_call(
        functools.partial(kernel, R, C, hops, line, chunks),
        out_shape=(
            jax.ShapeDtypeStruct((per_dev, local_rows), bf16),
            jax.ShapeDtypeStruct((rt, ct), jnp.float32),
        ),
        in_specs=[
            pl.BlockSpec(memory_space=pl.ANY),
            pl.BlockSpec(memory_space=pl.ANY),
            pl.BlockSpec(memory_space=pl.ANY),
            pl.BlockSpec(memory_space=pltpu.SMEM),
        ],
        out_specs=(pl.BlockSpec(memory_space=pl.ANY), pl.BlockSpec(memory_space=pltpu.VMEM)),
        scratch_shapes=[
            pltpu.VMEM((2, nb, half_nnz, B, B), bf16),
            pltpu.VMEM((half_nnz, nb), jnp.int32),
            pltpu.SMEM((2, half_nnz, nb), jnp.int32),
            pltpu.VMEM((V, local_rows), bf16),
            pltpu.VMEM((V, local_rows), bf16),
            pltpu.VMEM((K, bw), bf16),
            pltpu.VMEM((C, 2, K // 2, ct), bf16),
            pltpu.VMEM((G, K // 2, ct), bf16),
            pltpu.VMEM((R // 2, rt, ct), b_type),
            pltpu.VMEM((R, rt, ct), b_type),
        ]
        + [pltpu.VMEM((slots * nb + 1, vc, B), bf16)] * (2 * chunks)
        + [
            dma((2, chunks, 2, hops)), dma((2, chunks, 2, hops)),
            dma, dma, dma, dma, dma((5 + chunks,)),
            dma((chunks,)), dma((chunks,)),
            dma((chunks, G)), dma((chunks, G)),
            dma((G,)), dma((G,)),
            dma((R // 2, 2)), dma((R,)),
        ]
        + end_scratch,
        compiler_params=pltpu.CompilerParams(
            collective_id=0, has_side_effects=True, vmem_limit_bytes=60 * 1024 * 1024
        ),
    )(hamiltonian, pattern.T, vectors, spectrum)


def solution(mesh):
    in_specs = (
        P(("kpt", "row"), "rep", None, None),
        P("row", "rep"),
        P("col", ("kpt", "row")),
        P("kpt"),
    )
    out_specs = (P("col", ("kpt", "row")), P(("kpt", "row"), "col"))
    return jax.shard_map(
        functools.partial(on_device, mesh.shape["row"], mesh.shape["col"]),
        mesh=mesh, in_specs=in_specs, out_specs=out_specs, check_vma=False,
    )
```

```python
import functools

import jax
import jax.numpy as jnp
from jax import lax
from jax.experimental import pallas as pl
from jax.experimental.pallas import tpu as pltpu
from jax.sharding import PartitionSpec as P

MESH = pl.DeviceIdType.MESH
NT = (((1,), (1,)), ((), ()))
NN = (((1,), (0,)), ((), ()))
UNROLL = 8


def kernel(
    R, C, hops, line, chunks, h_ref, pat_ref, vec_ref, spec_ref, out_ref, gram_ref,
    hall, pvm, psm, stage, filt, gbuf, part, recv_a, send_b, recv_b, *rest,
):
    wins = rest[: 2 * chunks]
    (z_send, z_recv, h_send, h_recv, p_send, p_recv, loc, o_send, o_recv,
     g_send, g_recv, a_send, a_recv, b_send, b_recv) = rest[2 * chunks:2 * chunks + 15]
    extra = rest[2 * chunks + 15:]
    win1, win2 = wins[:chunks], wins[chunks:]
    ends = bool(extra)
    if ends:
        hx, pxv, pxs = extra[:3]
        s_out, s_in = extra[3:3 + chunks], extra[3 + chunks:3 + 2 * chunks]
        x_send, x_recv, w_send, w_recv, y_send, y_recv, px_send, px_recv, s_send, s_recv, e_send, e_recv = extra[3 + 2 * chunks:]
    k, r, c, p = (lax.axis_index(n) for n in ("kpt", "row", "col", "rep"))
    G = 2 * C
    g = c * 2 + p
    nb, half_nnz = h_ref.shape[0], h_ref.shape[1]
    B = h_ref.shape[2]
    V = stage.shape[0]
    vc = V // chunks
    bw = gbuf.shape[1]
    ct = part.shape[3]
    rt = send_b.shape[1]
    other = 1 - p

    local_v = pltpu.make_async_copy(vec_ref.at[pl.ds(pl.multiple_of(p * V, V), V)], stage, loc.at[0])
    local_v.start()
    local_h = pltpu.make_async_copy(h_ref, hall.at[p], loc.at[1])
    local_h.start()
    local_p = pltpu.make_async_copy(pat_ref, psm.at[p], loc.at[2])
    local_p.start()

    barrier = pltpu.get_barrier_semaphore()
    for j in range(1, 2 * R):
        o = lax.rem(r * 2 + p + j, 2 * R)
        pl.semaphore_signal(barrier, inc=1, device_id=(k, o // 2, c, lax.rem(o, 2)), device_id_type=MESH)
    for j in range(1, C):
        o = lax.rem(c + j, C)
        for q in range(2):
            pl.semaphore_signal(barrier, inc=1, device_id=(k, r, o, q), device_id_type=MESH)

    def slot(d):
        return r + d if line else 2 + d

    local_v.wait()
    own = slot(0) * nb

    def block_major(i, _):
        for q in range(chunks):
            win1[q][own + i] = stage[pl.ds(q * vc, vc), pl.ds(pl.multiple_of(i * B, B), B)]
        return 0

    lax.fori_loop(0, nb, block_major, 0)
    pl.semaphore_wait(barrier, 2 * R - 1 + 2 * (C - 1))

    def z_copy(step, q, way, h):
        win = (win1, win2)[step][q]
        sign = -1 if way == 0 else 1
        src = slot(sign * h)
        dst = src if line else slot(sign * (h + 1))
        target = r + 1 if way == 0 else r - 1
        target = lax.rem(target + R, R)
        return pltpu.make_async_remote_copy(
            src_ref=win.at[pl.ds(src * nb, nb)],
            dst_ref=win.at[pl.ds(dst * nb, nb)],
            send_sem=z_send.at[step, q, way, h],
            recv_sem=z_recv.at[step, q, way, h],
            device_id=(k, target, c, p),
            device_id_type=MESH,
        )

    def z_arrival(step, q, way, h):
        win = (win1, win2)[step][q]
        sign = -1 if way == 0 else 1
        dst = slot(sign * (h + 1))
        target = lax.rem((r - 1 if way == 0 else r + 1) + R, R)
        return pltpu.make_async_remote_copy(
            src_ref=win.at[pl.ds(dst * nb, nb)],
            dst_ref=win.at[pl.ds(dst * nb, nb)],
            send_sem=z_send.at[step, q, way, h],
            recv_sem=z_recv.at[step, q, way, h],
            device_id=(k, target, c, p),
            device_id_type=MESH,
        )

    if ends:
        outer = jnp.logical_or(r == 0, r == R - 1)
        inner = jnp.logical_not(outer)
        low = r < R // 2
        end = jnp.where(low, 0, R - 1)
        mate = jnp.where(low, 1 - r, 2 * R - 3 - r)
        zero_block = nb * R
        edge_near = jnp.where(low, nb, (R - 1) * nb - 1)
        edge_far = jnp.where(low, nb * R - 1, 0)

    def when(cond, fn):
        if line:
            pl.when(cond)(fn)
        else:
            fn()

    def sends(step, way, h):
        short = 1 if ends and step == 1 else 0
        if way == 0:
            return jnp.logical_and(r + 1 < R - short, r - h >= 0)
        return jnp.logical_and(r - 1 >= short, r + h < R)

    def receives(step, way, h):
        short = 1 if ends and step == 1 else 0
        if way == 0:
            return jnp.logical_and(r < R - short, r - 1 - h >= 0)
        return jnp.logical_and(r >= short, r + 1 + h < R)

    def z_start(step, q, h):
        for way in range(2):
            when(sends(step, way, h), lambda way=way: z_copy(step, q, way, h).start())

    def z_wait(step, q, h):
        for way in range(2):
            when(receives(step, way, h), lambda way=way: z_arrival(step, q, way, h).wait_recv())

    def z_forward(step, q, h):
        for way in range(2):
            when(receives(step, way, h - 1), lambda way=way: z_arrival(step, q, way, h - 1).wait_recv())
            when(sends(step, way, h), lambda way=way: z_copy(step, q, way, h).start())

    partner = (k, r, c, other)
    for q in range(chunks):
        z_start(0, q, 0)
    send_p = pltpu.make_async_remote_copy(pat_ref, pvm, p_send, p_recv, device_id=partner, device_id_type=MESH)
    send_p.start()
    send_h = pltpu.make_async_remote_copy(h_ref, hall.at[p], h_send, h_recv, device_id=partner, device_id_type=MESH)
    send_h.start()
    arrive_h = pltpu.make_async_remote_copy(h_ref, hall.at[other], h_send, h_recv, device_id=partner, device_id_type=MESH)
    if ends:
        pieces = 4
        piece = nb // (2 * pieces)

        def rows_of(half, j):
            return pl.ds((half * pieces + j) * piece, piece)

        def x_copy(j):
            return pltpu.make_async_remote_copy(
                h_ref.at[rows_of(c, j)], hx.at[rows_of(c, j)], x_send.at[j], x_recv.at[j],
                device_id=(k, mate, c, p), device_id_type=MESH,
            )

        def w_copy(half, j):
            return pltpu.make_async_remote_copy(
                hx.at[rows_of(half, j)], hx.at[rows_of(half, j)], w_send.at[j], w_recv.at[j],
                device_id=(k, r, 1 - c, p), device_id_type=MESH,
            )

        def y_copy(half, n, j):
            return pltpu.make_async_remote_copy(
                hx.at[rows_of(half, j)], hx.at[rows_of(half, j)], y_send.at[n, j], y_recv.at[n, j],
                device_id=partner, device_id_type=MESH,
            )

        def px_copy(q):
            return pltpu.make_async_remote_copy(
                pat_ref, pxv, px_send.at[q], px_recv, device_id=(k, mate, c, q), device_id_type=MESH,
            )

        from_end = jnp.logical_and(outer, p == 1)
        relay = jnp.logical_and(inner, p == 1)
        relayed = jnp.logical_and(inner, p == 0)

        @pl.when(from_end)
        def _():
            for q in range(2):
                px_copy(q).start()
            for j in range(pieces):
                x_copy(j).start()

        for q in range(chunks):
            win2[q][zero_block] = jnp.zeros((vc, B), jnp.bfloat16)

    send_p.wait_recv()
    other_p = pltpu.make_async_copy(pvm, psm.at[other], loc.at[3])
    other_p.start()

    for h in range(1, hops):
        for q in range(chunks):
            z_forward(0, q, h)

    local_h.wait()
    local_p.wait()
    other_p.wait()
    arrive_h.wait_recv()

    centre = spec_ref[0]
    inverse = 1.0 / jnp.full((vc, B), spec_ref[1], jnp.float32)
    total = nb * R

    def index(half, i, s):
        named = psm[half, s, i]
        if line:
            return named
        return lax.rem(named - (r - 2) * nb + total, total)

    def turn(i, _):
        for half in range(2):
            for s in range(half_nnz):
                hall[half, i, s] = hall[half, i, s].T
        return 0

    lax.fori_loop(0, nb, turn, 0, unroll=2)

    def product(win, i, held_back=False):
        def place(half, s):
            named = index(half, i, s)
            if held_back and half == 1:
                away = jnp.logical_and(outer, named // nb != r)
                named = jnp.where(away, zero_block, named)
            return named

        picked = [win[place(half, s)] for half in range(2) for s in range(half_nnz)]
        stored = [hall[half, i].reshape(half_nnz * B, B) for half in range(2)]
        return jnp.dot(
            jnp.concatenate(picked, axis=1), jnp.concatenate(stored, axis=0),
            preferred_element_type=jnp.float32,
        )

    if ends:
        @pl.when(relay)
        def _():
            for j in range(pieces):
                x_copy(j).wait_recv()
                w_copy(c, j).start()
                y_copy(c, 0, j).start()

    if ends:
        @pl.when(inner)
        def _():
            def clear(i, _):
                for q in range(chunks):
                    s_in[q][i] = jnp.zeros((vc, B), jnp.bfloat16)
                return 0

            lax.fori_loop(0, nb, clear, 0)

    for q in range(chunks):
        z_wait(0, q, hops - 1)

        def first_row(i, _, q=q):
            start = win1[q][own + i].astype(jnp.float32)
            win2[q][own + i] = ((product(win1[q], i) - centre * start) * inverse).astype(jnp.bfloat16)
            return 0

        lax.fori_loop(0, nb, first_row, 0, unroll=UNROLL)
        z_start(1, q, 0)

    if ends:
        @pl.when(inner)
        def _():
            px_copy(0).wait_recv()
            names = pltpu.make_async_copy(pxv, pxs, loc.at[4 + chunks])
            names.start()
            names.wait()

        @pl.when(relay)
        def _():
            for j in range(pieces):
                w_copy(1 - c, j).wait_recv()
                y_copy(1 - c, 1, j).start()
            for j in range(pieces):
                w_copy(c, j).wait_send()
                y_copy(c, 0, j).wait_send()
                y_copy(1 - c, 1, j).wait_send()

        @pl.when(relayed)
        def _():
            for j in range(pieces):
                y_copy(c, 0, j).wait_recv()
                y_copy(1 - c, 1, j).wait_recv()

        @pl.when(inner)
        def _():
            def turn_x(i, _):
                for s in range(half_nnz):
                    hx[i, s] = hx[i, s].T
                return 0

            lax.fori_loop(0, nb, turn_x, 0, unroll=2)

        def s_copy(q):
            return pltpu.make_async_remote_copy(
                s_out[q], s_in[q], s_send.at[q], s_recv.at[q],
                device_id=(k, mate, c, p), device_id_type=MESH,
            )

        def e_copy(q, which):
            block = pl.ds((edge_near, edge_far)[which], 1)
            return pltpu.make_async_remote_copy(
                win2[q].at[block], win2[q].at[block], e_send.at[q, which], e_recv.at[q, which],
                device_id=(k, mate, c, p), device_id_type=MESH,
            )

    hops2 = hops - 1 if ends else hops
    for h in range(1, hops2):
        for q in range(chunks):
            z_forward(1, q, h)

    def group(j):
        o = lax.rem(g + j, G)
        return o, (k, r, o // 2, lax.rem(o, 2))

    def vec_row(gi, q):
        return pl.ds(pl.multiple_of(gi * V + q * vc, vc), vc)

    tail = []
    for q in range(chunks):
        z_wait(1, q, hops2 - 1)
        if ends:
            @pl.when(inner)
            def _(q=q):
                for which in range(2):
                    e_copy(q, which).start()

                def end_row(i, _):
                    picked = []
                    for s in range(half_nnz):
                        named = pxs[s, i]
                        picked.append(win2[q][jnp.where(named // nb == end, zero_block, named)])
                    s_out[q][i] = jnp.dot(
                        jnp.concatenate(picked, axis=1), hx[i].reshape(half_nnz * B, B),
                        preferred_element_type=jnp.float32,
                    ).astype(jnp.bfloat16)
                    return 0

                lax.fori_loop(0, nb, end_row, 0, unroll=UNROLL)
                s_copy(q).start()

            @pl.when(outer)
            def _(q=q):
                for which in range(2):
                    e_copy(q, which).wait_recv()
                s_copy(q).wait_recv()

        def filtered_row(i, _, q=q):
            first = win2[q][own + i].astype(jnp.float32)
            start = win1[q][own + i].astype(jnp.float32)
            sums = product(win2[q], i, ends)
            if ends:
                sums = sums + s_in[q][i].astype(jnp.float32)
            value = 2.0 * ((sums - centre * first) * inverse) - start
            filt[pl.ds(q * vc, vc), pl.ds(pl.multiple_of(i * B, B), B)] = value.astype(jnp.bfloat16)
            return 0

        lax.fori_loop(0, nb, filtered_row, 0, unroll=UNROLL)
        for j in range(1, G):
            o, device = group(j)
            copy = pltpu.make_async_remote_copy(
                filt.at[pl.ds(q * vc, vc), pl.ds(pl.multiple_of(o * bw, bw), bw)],
                gbuf.at[vec_row(g, q)],
                g_send.at[q, j], g_recv.at[q, j], device_id=device, device_id_type=MESH,
            )
            copy.start()
            tail.append(copy)
        gbuf[vec_row(g, q), :] = filt[pl.ds(q * vc, vc), pl.ds(pl.multiple_of(g * bw, bw), bw)]
        rows = pl.ds(pl.multiple_of(p * V + q * vc, vc), vc)
        keep = pltpu.make_async_copy(filt.at[pl.ds(q * vc, vc)], out_ref.at[rows], loc.at[4 + q])
        keep.start()
        copy = pltpu.make_async_remote_copy(
            filt.at[pl.ds(q * vc, vc)], out_ref.at[rows], o_send.at[q], o_recv.at[q],
            device_id=partner, device_id_type=MESH,
        )
        copy.start()
        tail.append(copy)

    for q in range(chunks):
        for j in range(1, G):
            source = lax.rem(g - j + G, G)
            pltpu.make_async_remote_copy(
                gbuf.at[vec_row(source, q)], gbuf.at[vec_row(source, q)],
                g_send.at[q, j], g_recv.at[q, j], device_id=group(j)[1], device_id_type=MESH,
            ).wait_recv()

    everything = gbuf[...]
    for cc in range(C):
        tile = lax.dot_general(
            everything, gbuf[pl.ds(cc * ct, ct), :], NT, preferred_element_type=jnp.float32
        ).astype(jnp.bfloat16)
        part[cc, 0] = tile[: rt * R // 2]
        part[cc, 1] = tile[rt * R // 2:]
    for j in range(1, G):
        o, device = group(j)
        copy = pltpu.make_async_remote_copy(
            part.at[o // 2, lax.rem(o, 2)], recv_a.at[g], a_send.at[j], a_recv.at[j],
            device_id=device, device_id_type=MESH,
        )
        copy.start()
        tail.append(copy)
    recv_a[g] = part[c, p]
    for j in range(1, G):
        source = lax.rem(g - j + G, G)
        pltpu.make_async_remote_copy(
            recv_a.at[source], recv_a.at[source], a_send.at[j], a_recv.at[j],
            device_id=group(j)[1], device_id_type=MESH,
        ).wait_recv()
    summed = recv_a[0].astype(jnp.float32)
    for j in range(1, G):
        summed = summed + recv_a[j].astype(jnp.float32)
    for j in range(R // 2):
        send_b[j] = summed[j * rt:(j + 1) * rt].astype(send_b.dtype)

    def b_copy(j, q):
        return pltpu.make_async_remote_copy(
            send_b.at[j], recv_b.at[r], b_send.at[j, q], b_recv.at[r],
            device_id=(k, p * (R // 2) + j, c, q), device_id_type=MESH,
        )

    def b_elsewhere(j, q):
        return jnp.logical_or(r != p * (R // 2) + j, p != q)

    for j in range(R // 2):
        for q in range(2):
            pl.when(b_elsewhere(j, q))(lambda j=j, q=q: b_copy(j, q).start())
        pl.when(r == p * (R // 2) + j)(lambda j=j: recv_b.__setitem__(r, send_b[j]))
    mine = r // (R // 2)
    for source in range(R):
        arrive = pltpu.make_async_remote_copy(
            recv_b.at[source], recv_b.at[source], b_send.at[0, 0], b_recv.at[source],
            device_id=(k, source, c, mine), device_id_type=MESH,
        )
        pl.when(jnp.logical_or(r != source, p != mine))(lambda arrive=arrive: arrive.wait_recv())
    gram = recv_b[0].astype(jnp.float32)
    for source in range(1, R):
        gram = gram + recv_b[source].astype(jnp.float32)
    gram_ref[...] = gram * (1.0 / (total * B))

    for step in range(2):
        for q in range(chunks):
            for h in range(hops):
                for way in range(2):
                    when(sends(step, way, h), lambda a=(step, q, way, h): z_copy(*a).wait_send())
    if ends:
        @pl.when(from_end)
        def _():
            for j in range(2):
                px_copy(j).wait_send()
            for j in range(pieces):
                x_copy(j).wait_send()

        @pl.when(inner)
        def _():
            for q in range(chunks):
                s_copy(q).wait_send()
                for which in range(2):
                    e_copy(q, which).wait_send()
    send_p.wait_send()
    send_h.wait_send()
    for copy in tail:
        copy.wait_send()
    for j in range(R // 2):
        for q in range(2):
            pl.when(b_elsewhere(j, q))(lambda j=j, q=q: b_copy(j, q).wait_send())
    for q in range(chunks):
        rows = pl.ds(pl.multiple_of(p * V + q * vc, vc), vc)
        pltpu.make_async_copy(filt.at[pl.ds(q * vc, vc)], out_ref.at[rows], loc.at[4 + q]).wait()
        theirs = pl.ds(pl.multiple_of(other * V + q * vc, vc), vc)
        pltpu.make_async_remote_copy(
            filt.at[pl.ds(q * vc, vc)], out_ref.at[theirs], o_send.at[q], o_recv.at[q],
            device_id=partner, device_id_type=MESH,
        ).wait_recv()


def on_device(R, C, hamiltonian, pattern, vectors, spectrum):
    nb, half_nnz, B, _ = hamiltonian.shape
    per_dev, local_rows = vectors.shape
    line = R <= 4
    hops = R - 1 if line else 2
    slots = R if line else 5
    V = per_dev // 2
    chunks = 4 if V % 64 == 0 else max(V // 16, 1)
    vc = V // chunks
    G = 2 * C
    K = per_dev * C
    bw = local_rows // G
    rt, ct = K // R, per_dev
    b_type = jnp.bfloat16 if rt % 16 == 0 else jnp.float32
    bf16 = jnp.bfloat16
    dma = pltpu.SemaphoreType.DMA
    end_scratch = []
    if R == 4 and C == 2:
        end_scratch = [
            pltpu.VMEM((nb, half_nnz, B, B), bf16),
            pltpu.VMEM((half_nnz, nb), jnp.int32),
            pltpu.SMEM((half_nnz, nb), jnp.int32),
        ] + [pltpu.VMEM((nb, vc, B), bf16)] * (2 * chunks) + [
            dma((4,)), dma((4,)), dma((4,)), dma((4,)), dma((2, 4)), dma((2, 4)), dma((2,)), dma,
            dma((chunks,)), dma((chunks,)), dma((chunks, 2)), dma((chunks, 2)),
        ]
    return pl.pallas_call(
        functools.partial(kernel, R, C, hops, line, chunks),
        out_shape=(
            jax.ShapeDtypeStruct((per_dev, local_rows), bf16),
            jax.ShapeDtypeStruct((rt, ct), jnp.float32),
        ),
        in_specs=[
            pl.BlockSpec(memory_space=pl.ANY),
            pl.BlockSpec(memory_space=pl.ANY),
            pl.BlockSpec(memory_space=pl.ANY),
            pl.BlockSpec(memory_space=pltpu.SMEM),
        ],
        out_specs=(pl.BlockSpec(memory_space=pl.ANY), pl.BlockSpec(memory_space=pltpu.VMEM)),
        scratch_shapes=[
            pltpu.VMEM((2, nb, half_nnz, B, B), bf16),
            pltpu.VMEM((half_nnz, nb), jnp.int32),
            pltpu.SMEM((2, half_nnz, nb), jnp.int32),
            pltpu.VMEM((V, local_rows), bf16),
            pltpu.VMEM((V, local_rows), bf16),
            pltpu.VMEM((K, bw), bf16),
            pltpu.VMEM((C, 2, K // 2, ct), bf16),
            pltpu.VMEM((G, K // 2, ct), bf16),
            pltpu.VMEM((R // 2, rt, ct), b_type),
            pltpu.VMEM((R, rt, ct), b_type),
        ]
        + [pltpu.VMEM((slots * nb + 1, vc, B), bf16)] * (2 * chunks)
        + [
            dma((2, chunks, 2, hops)), dma((2, chunks, 2, hops)),
            dma, dma, dma, dma, dma((5 + chunks,)),
            dma((chunks,)), dma((chunks,)),
            dma((chunks, G)), dma((chunks, G)),
            dma((G,)), dma((G,)),
            dma((R // 2, 2)), dma((R,)),
        ]
        + end_scratch,
        compiler_params=pltpu.CompilerParams(
            collective_id=0, has_side_effects=True, vmem_limit_bytes=60 * 1024 * 1024
        ),
    )(hamiltonian, pattern.T, vectors, spectrum)


def solution(mesh):
    in_specs = (
        P(("kpt", "row"), "rep", None, None),
        P("row", "rep"),
        P("col", ("kpt", "row")),
        P("kpt"),
    )
    out_specs = (P("col", ("kpt", "row")), P(("kpt", "row"), "col"))
    return jax.shard_map(
        functools.partial(on_device, mesh.shape["row"], mesh.shape["col"]),
        mesh=mesh, in_specs=in_specs, out_specs=out_specs, check_vma=False,
    )
```

```python
import functools

import jax
import jax.numpy as jnp
from jax import lax
from jax.experimental import pallas as pl
from jax.experimental.pallas import tpu as pltpu
from jax.sharding import PartitionSpec as P

MESH = pl.DeviceIdType.MESH
NT = (((1,), (1,)), ((), ()))
NN = (((1,), (0,)), ((), ()))
UNROLL = 8


def kernel(
    R, C, hops, line, chunks, h_ref, pat_ref, vec_ref, spec_ref, out_ref, gram_ref,
    hall, pvm, psm, stage, filt, gbuf, part, recv_a, send_b, recv_b, *rest,
):
    wins = rest[: 2 * chunks]
    (z_send, z_recv, h_send, h_recv, p_send, p_recv, loc, o_send, o_recv,
     g_send, g_recv, a_send, a_recv, b_send, b_recv) = rest[2 * chunks:2 * chunks + 15]
    extra = rest[2 * chunks + 15:]
    win1, win2 = wins[:chunks], wins[chunks:]
    ends = bool(extra)
    if ends:
        hx, pxv, pxs = extra[:3]
        s_out, s_in = extra[3:3 + chunks], extra[3 + chunks:3 + 2 * chunks]
        x_send, x_recv, w_send, w_recv, y_send, y_recv, px_send, px_recv, s_send, s_recv, e_send, e_recv = extra[3 + 2 * chunks:]
    k, r, c, p = (lax.axis_index(n) for n in ("kpt", "row", "col", "rep"))
    G = 2 * C
    g = c * 2 + p
    nb, half_nnz = h_ref.shape[0], h_ref.shape[1]
    B = h_ref.shape[2]
    V = stage.shape[0]
    vc = V // chunks
    bw = gbuf.shape[1]
    ct = part.shape[3]
    rt = send_b.shape[1]
    other = 1 - p

    local_v = pltpu.make_async_copy(vec_ref.at[pl.ds(pl.multiple_of(p * V, V), V)], stage, loc.at[0])
    local_v.start()
    local_h = pltpu.make_async_copy(h_ref, hall.at[p], loc.at[1])
    local_h.start()
    local_p = pltpu.make_async_copy(pat_ref, psm.at[p], loc.at[2])
    local_p.start()

    barrier = pltpu.get_barrier_semaphore()
    for j in range(1, 2 * R):
        o = lax.rem(r * 2 + p + j, 2 * R)
        pl.semaphore_signal(barrier, inc=1, device_id=(k, o // 2, c, lax.rem(o, 2)), device_id_type=MESH)
    for j in range(1, C):
        o = lax.rem(c + j, C)
        for q in range(2):
            pl.semaphore_signal(barrier, inc=1, device_id=(k, r, o, q), device_id_type=MESH)

    def slot(d):
        return r + d if line else 2 + d

    local_v.wait()
    own = slot(0) * nb

    def block_major(i, _):
        for q in range(chunks):
            win1[q][own + i] = stage[pl.ds(q * vc, vc), pl.ds(pl.multiple_of(i * B, B), B)]
        return 0

    lax.fori_loop(0, nb, block_major, 0)
    pl.semaphore_wait(barrier, 2 * R - 1 + 2 * (C - 1))

    def z_copy(step, q, way, h):
        win = (win1, win2)[step][q]
        sign = -1 if way == 0 else 1
        src = slot(sign * h)
        dst = src if line else slot(sign * (h + 1))
        target = r + 1 if way == 0 else r - 1
        target = lax.rem(target + R, R)
        return pltpu.make_async_remote_copy(
            src_ref=win.at[pl.ds(src * nb, nb)],
            dst_ref=win.at[pl.ds(dst * nb, nb)],
            send_sem=z_send.at[step, q, way, h],
            recv_sem=z_recv.at[step, q, way, h],
            device_id=(k, target, c, p),
            device_id_type=MESH,
        )

    def z_arrival(step, q, way, h):
        win = (win1, win2)[step][q]
        sign = -1 if way == 0 else 1
        dst = slot(sign * (h + 1))
        target = lax.rem((r - 1 if way == 0 else r + 1) + R, R)
        return pltpu.make_async_remote_copy(
            src_ref=win.at[pl.ds(dst * nb, nb)],
            dst_ref=win.at[pl.ds(dst * nb, nb)],
            send_sem=z_send.at[step, q, way, h],
            recv_sem=z_recv.at[step, q, way, h],
            device_id=(k, target, c, p),
            device_id_type=MESH,
        )

    if ends:
        outer = jnp.logical_or(r == 0, r == R - 1)
        inner = jnp.logical_not(outer)
        low = r < R // 2
        end = jnp.where(low, 0, R - 1)
        mate = jnp.where(low, 1 - r, 2 * R - 3 - r)
        zero_block = nb * R
        edge_near = jnp.where(low, nb, (R - 1) * nb - 1)
        edge_far = jnp.where(low, nb * R - 1, 0)

    def when(cond, fn):
        if line:
            pl.when(cond)(fn)
        else:
            fn()

    def sends(step, way, h):
        short = 1 if ends and step == 1 else 0
        if way == 0:
            return jnp.logical_and(r + 1 < R - short, r - h >= 0)
        return jnp.logical_and(r - 1 >= short, r + h < R)

    def receives(step, way, h):
        short = 1 if ends and step == 1 else 0
        if way == 0:
            return jnp.logical_and(r < R - short, r - 1 - h >= 0)
        return jnp.logical_and(r >= short, r + 1 + h < R)

    def z_start(step, q, h):
        for way in range(2):
            when(sends(step, way, h), lambda way=way: z_copy(step, q, way, h).start())

    def z_wait(step, q, h):
        for way in range(2):
            when(receives(step, way, h), lambda way=way: z_arrival(step, q, way, h).wait_recv())

    def z_forward(step, q, h):
        for way in range(2):
            when(receives(step, way, h - 1), lambda way=way: z_arrival(step, q, way, h - 1).wait_recv())
            when(sends(step, way, h), lambda way=way: z_copy(step, q, way, h).start())

    partner = (k, r, c, other)
    for q in range(chunks):
        z_start(0, q, 0)
    send_p = pltpu.make_async_remote_copy(pat_ref, pvm, p_send, p_recv, device_id=partner, device_id_type=MESH)
    send_p.start()
    send_h = pltpu.make_async_remote_copy(h_ref, hall.at[p], h_send, h_recv, device_id=partner, device_id_type=MESH)
    send_h.start()
    arrive_h = pltpu.make_async_remote_copy(h_ref, hall.at[other], h_send, h_recv, device_id=partner, device_id_type=MESH)
    if ends:
        pieces = 4
        piece = nb // (2 * pieces)

        def rows_of(half, j):
            return pl.ds((half * pieces + j) * piece, piece)

        def x_copy(j):
            return pltpu.make_async_remote_copy(
                h_ref.at[rows_of(c, j)], hx.at[rows_of(c, j)], x_send.at[j], x_recv.at[j],
                device_id=(k, mate, c, p), device_id_type=MESH,
            )

        def w_copy(half, j):
            return pltpu.make_async_remote_copy(
                hx.at[rows_of(half, j)], hx.at[rows_of(half, j)], w_send.at[j], w_recv.at[j],
                device_id=(k, r, 1 - c, p), device_id_type=MESH,
            )

        def y_copy(half, n, j):
            return pltpu.make_async_remote_copy(
                hx.at[rows_of(half, j)], hx.at[rows_of(half, j)], y_send.at[n, j], y_recv.at[n, j],
                device_id=partner, device_id_type=MESH,
            )

        def px_copy(q):
            return pltpu.make_async_remote_copy(
                pat_ref, pxv, px_send.at[q], px_recv, device_id=(k, mate, c, q), device_id_type=MESH,
            )

        from_end = jnp.logical_and(outer, p == 1)
        relay = jnp.logical_and(inner, p == 1)
        relayed = jnp.logical_and(inner, p == 0)

        @pl.when(from_end)
        def _():
            for q in range(2):
                px_copy(q).start()
            for j in range(pieces):
                x_copy(j).start()

        for q in range(chunks):
            win2[q][zero_block] = jnp.zeros((vc, B), jnp.bfloat16)

    send_p.wait_recv()
    other_p = pltpu.make_async_copy(pvm, psm.at[other], loc.at[3])
    other_p.start()

    for h in range(1, hops):
        for q in range(chunks):
            z_forward(0, q, h)

    local_h.wait()
    local_p.wait()
    other_p.wait()
    arrive_h.wait_recv()

    centre = spec_ref[0]
    inverse = 1.0 / jnp.full((vc, B), spec_ref[1], jnp.float32)
    total = nb * R

    def index(half, i, s):
        named = psm[half, s, i]
        if line:
            return named
        return lax.rem(named - (r - 2) * nb + total, total)

    def turn(i, _):
        for half in range(2):
            for s in range(half_nnz):
                hall[half, i, s] = hall[half, i, s].T
        return 0

    lax.fori_loop(0, nb, turn, 0, unroll=2)

    def product(win, i, held_back=False):
        def place(half, s):
            named = index(half, i, s)
            if held_back and half == 1:
                away = jnp.logical_and(outer, named // nb != r)
                named = jnp.where(away, zero_block, named)
            return named

        picked = [win[place(half, s)] for half in range(2) for s in range(half_nnz)]
        stored = [hall[half, i].reshape(half_nnz * B, B) for half in range(2)]
        return jnp.dot(
            jnp.concatenate(picked, axis=1), jnp.concatenate(stored, axis=0),
            preferred_element_type=jnp.float32,
        )

    if ends:
        @pl.when(inner)
        def _():
            def clear(i, _):
                for q in range(chunks):
                    s_in[q][i] = jnp.zeros((vc, B), jnp.bfloat16)
                return 0

            lax.fori_loop(0, nb, clear, 0)

    for q in range(chunks):
        if ends:
            @pl.when(relay)
            def _(q=q):
                for j in range(q * pieces // chunks, (q + 1) * pieces // chunks):
                    x_copy(j).wait_recv()
                    w_copy(c, j).start()
                    y_copy(c, 0, j).start()

        z_wait(0, q, hops - 1)

        def first_row(i, _, q=q):
            start = win1[q][own + i].astype(jnp.float32)
            win2[q][own + i] = ((product(win1[q], i) - centre * start) * inverse).astype(jnp.bfloat16)
            return 0

        lax.fori_loop(0, nb, first_row, 0, unroll=UNROLL)
        z_start(1, q, 0)

    if ends:
        @pl.when(inner)
        def _():
            px_copy(0).wait_recv()
            names = pltpu.make_async_copy(pxv, pxs, loc.at[4 + chunks])
            names.start()
            names.wait()

        @pl.when(relay)
        def _():
            for j in range(pieces):
                w_copy(1 - c, j).wait_recv()
                y_copy(1 - c, 1, j).start()
            for j in range(pieces):
                w_copy(c, j).wait_send()
                y_copy(c, 0, j).wait_send()
                y_copy(1 - c, 1, j).wait_send()

        @pl.when(relayed)
        def _():
            for j in range(pieces):
                y_copy(c, 0, j).wait_recv()
                y_copy(1 - c, 1, j).wait_recv()

        @pl.when(inner)
        def _():
            def turn_x(i, _):
                for s in range(half_nnz):
                    hx[i, s] = hx[i, s].T
                return 0

            lax.fori_loop(0, nb, turn_x, 0, unroll=2)

        def s_copy(q):
            return pltpu.make_async_remote_copy(
                s_out[q], s_in[q], s_send.at[q], s_recv.at[q],
                device_id=(k, mate, c, p), device_id_type=MESH,
            )

        def e_copy(q, which):
            block = pl.ds((edge_near, edge_far)[which], 1)
            return pltpu.make_async_remote_copy(
                win2[q].at[block], win2[q].at[block], e_send.at[q, which], e_recv.at[q, which],
                device_id=(k, mate, c, p), device_id_type=MESH,
            )

    hops2 = hops - 1 if ends else hops
    for h in range(1, hops2):
        for q in range(chunks):
            z_forward(1, q, h)

    def group(j):
        o = lax.rem(g + j, G)
        return o, (k, r, o // 2, lax.rem(o, 2))

    def vec_row(gi, q):
        return pl.ds(pl.multiple_of(gi * V + q * vc, vc), vc)

    tail = []
    for q in range(chunks):
        z_wait(1, q, hops2 - 1)
        if ends:
            @pl.when(inner)
            def _(q=q):
                for which in range(2):
                    e_copy(q, which).start()

                def end_row(i, _):
                    picked = []
                    for s in range(half_nnz):
                        named = pxs[s, i]
                        picked.append(win2[q][jnp.where(named // nb == end, zero_block, named)])
                    s_out[q][i] = jnp.dot(
                        jnp.concatenate(picked, axis=1), hx[i].reshape(half_nnz * B, B),
                        preferred_element_type=jnp.float32,
                    ).astype(jnp.bfloat16)
                    return 0

                lax.fori_loop(0, nb, end_row, 0, unroll=UNROLL)
                s_copy(q).start()

            @pl.when(outer)
            def _(q=q):
                for which in range(2):
                    e_copy(q, which).wait_recv()
                s_copy(q).wait_recv()

        def filtered_row(i, _, q=q):
            first = win2[q][own + i].astype(jnp.float32)
            start = win1[q][own + i].astype(jnp.float32)
            sums = product(win2[q], i, ends)
            if ends:
                sums = sums + s_in[q][i].astype(jnp.float32)
            value = 2.0 * ((sums - centre * first) * inverse) - start
            filt[pl.ds(q * vc, vc), pl.ds(pl.multiple_of(i * B, B), B)] = value.astype(jnp.bfloat16)
            return 0

        lax.fori_loop(0, nb, filtered_row, 0, unroll=UNROLL)
        for j in range(1, G):
            o, device = group(j)
            copy = pltpu.make_async_remote_copy(
                filt.at[pl.ds(q * vc, vc), pl.ds(pl.multiple_of(o * bw, bw), bw)],
                gbuf.at[vec_row(g, q)],
                g_send.at[q, j], g_recv.at[q, j], device_id=device, device_id_type=MESH,
            )
            copy.start()
            tail.append(copy)
        gbuf[vec_row(g, q), :] = filt[pl.ds(q * vc, vc), pl.ds(pl.multiple_of(g * bw, bw), bw)]
        rows = pl.ds(pl.multiple_of(p * V + q * vc, vc), vc)
        keep = pltpu.make_async_copy(filt.at[pl.ds(q * vc, vc)], out_ref.at[rows], loc.at[4 + q])
        keep.start()
        copy = pltpu.make_async_remote_copy(
            filt.at[pl.ds(q * vc, vc)], out_ref.at[rows], o_send.at[q], o_recv.at[q],
            device_id=partner, device_id_type=MESH,
        )
        copy.start()
        tail.append(copy)

    for q in range(chunks):
        for j in range(1, G):
            source = lax.rem(g - j + G, G)
            pltpu.make_async_remote_copy(
                gbuf.at[vec_row(source, q)], gbuf.at[vec_row(source, q)],
                g_send.at[q, j], g_recv.at[q, j], device_id=group(j)[1], device_id_type=MESH,
            ).wait_recv()

    everything = gbuf[...]
    for cc in range(C):
        tile = lax.dot_general(
            everything, gbuf[pl.ds(cc * ct, ct), :], NT, preferred_element_type=jnp.float32
        ).astype(jnp.bfloat16)
        part[cc, 0] = tile[: rt * R // 2]
        part[cc, 1] = tile[rt * R // 2:]
    for j in range(1, G):
        o, device = group(j)
        copy = pltpu.make_async_remote_copy(
            part.at[o // 2, lax.rem(o, 2)], recv_a.at[g], a_send.at[j], a_recv.at[j],
            device_id=device, device_id_type=MESH,
        )
        copy.start()
        tail.append(copy)
    recv_a[g] = part[c, p]
    for j in range(1, G):
        source = lax.rem(g - j + G, G)
        pltpu.make_async_remote_copy(
            recv_a.at[source], recv_a.at[source], a_send.at[j], a_recv.at[j],
            device_id=group(j)[1], device_id_type=MESH,
        ).wait_recv()
    summed = recv_a[0].astype(jnp.float32)
    for j in range(1, G):
        summed = summed + recv_a[j].astype(jnp.float32)
    for j in range(R // 2):
        send_b[j] = summed[j * rt:(j + 1) * rt].astype(send_b.dtype)

    def b_copy(j, q):
        return pltpu.make_async_remote_copy(
            send_b.at[j], recv_b.at[r], b_send.at[j, q], b_recv.at[r],
            device_id=(k, p * (R // 2) + j, c, q), device_id_type=MESH,
        )

    def b_elsewhere(j, q):
        return jnp.logical_or(r != p * (R // 2) + j, p != q)

    for j in range(R // 2):
        for q in range(2):
            pl.when(b_elsewhere(j, q))(lambda j=j, q=q: b_copy(j, q).start())
        pl.when(r == p * (R // 2) + j)(lambda j=j: recv_b.__setitem__(r, send_b[j]))
    mine = r // (R // 2)
    for source in range(R):
        arrive = pltpu.make_async_remote_copy(
            recv_b.at[source], recv_b.at[source], b_send.at[0, 0], b_recv.at[source],
            device_id=(k, source, c, mine), device_id_type=MESH,
        )
        pl.when(jnp.logical_or(r != source, p != mine))(lambda arrive=arrive: arrive.wait_recv())
    gram = recv_b[0].astype(jnp.float32)
    for source in range(1, R):
        gram = gram + recv_b[source].astype(jnp.float32)
    gram_ref[...] = gram * (1.0 / (total * B))

    for step in range(2):
        for q in range(chunks):
            for h in range(hops):
                for way in range(2):
                    when(sends(step, way, h), lambda a=(step, q, way, h): z_copy(*a).wait_send())
    if ends:
        @pl.when(from_end)
        def _():
            for j in range(2):
                px_copy(j).wait_send()
            for j in range(pieces):
                x_copy(j).wait_send()

        @pl.when(inner)
        def _():
            for q in range(chunks):
                s_copy(q).wait_send()
                for which in range(2):
                    e_copy(q, which).wait_send()
    send_p.wait_send()
    send_h.wait_send()
    for copy in tail:
        copy.wait_send()
    for j in range(R // 2):
        for q in range(2):
            pl.when(b_elsewhere(j, q))(lambda j=j, q=q: b_copy(j, q).wait_send())
    for q in range(chunks):
        rows = pl.ds(pl.multiple_of(p * V + q * vc, vc), vc)
        pltpu.make_async_copy(filt.at[pl.ds(q * vc, vc)], out_ref.at[rows], loc.at[4 + q]).wait()
        theirs = pl.ds(pl.multiple_of(other * V + q * vc, vc), vc)
        pltpu.make_async_remote_copy(
            filt.at[pl.ds(q * vc, vc)], out_ref.at[theirs], o_send.at[q], o_recv.at[q],
            device_id=partner, device_id_type=MESH,
        ).wait_recv()


def on_device(R, C, hamiltonian, pattern, vectors, spectrum):
    nb, half_nnz, B, _ = hamiltonian.shape
    per_dev, local_rows = vectors.shape
    line = R <= 4
    hops = R - 1 if line else 2
    slots = R if line else 5
    V = per_dev // 2
    chunks = 4 if V % 64 == 0 else max(V // 16, 1)
    vc = V // chunks
    G = 2 * C
    K = per_dev * C
    bw = local_rows // G
    rt, ct = K // R, per_dev
    b_type = jnp.bfloat16 if rt % 16 == 0 else jnp.float32
    bf16 = jnp.bfloat16
    dma = pltpu.SemaphoreType.DMA
    end_scratch = []
    if R == 4 and C == 2:
        end_scratch = [
            pltpu.VMEM((nb, half_nnz, B, B), bf16),
            pltpu.VMEM((half_nnz, nb), jnp.int32),
            pltpu.SMEM((half_nnz, nb), jnp.int32),
        ] + [pltpu.VMEM((nb, vc, B), bf16)] * (2 * chunks) + [
            dma((4,)), dma((4,)), dma((4,)), dma((4,)), dma((2, 4)), dma((2, 4)), dma((2,)), dma,
            dma((chunks,)), dma((chunks,)), dma((chunks, 2)), dma((chunks, 2)),
        ]
    return pl.pallas_call(
        functools.partial(kernel, R, C, hops, line, chunks),
        out_shape=(
            jax.ShapeDtypeStruct((per_dev, local_rows), bf16),
            jax.ShapeDtypeStruct((rt, ct), jnp.float32),
        ),
        in_specs=[
            pl.BlockSpec(memory_space=pl.ANY),
            pl.BlockSpec(memory_space=pl.ANY),
            pl.BlockSpec(memory_space=pl.ANY),
            pl.BlockSpec(memory_space=pltpu.SMEM),
        ],
        out_specs=(pl.BlockSpec(memory_space=pl.ANY), pl.BlockSpec(memory_space=pltpu.VMEM)),
        scratch_shapes=[
            pltpu.VMEM((2, nb, half_nnz, B, B), bf16),
            pltpu.VMEM((half_nnz, nb), jnp.int32),
            pltpu.SMEM((2, half_nnz, nb), jnp.int32),
            pltpu.VMEM((V, local_rows), bf16),
            pltpu.VMEM((V, local_rows), bf16),
            pltpu.VMEM((K, bw), bf16),
            pltpu.VMEM((C, 2, K // 2, ct), bf16),
            pltpu.VMEM((G, K // 2, ct), bf16),
            pltpu.VMEM((R // 2, rt, ct), b_type),
            pltpu.VMEM((R, rt, ct), b_type),
        ]
        + [pltpu.VMEM((slots * nb + 1, vc, B), bf16)] * (2 * chunks)
        + [
            dma((2, chunks, 2, hops)), dma((2, chunks, 2, hops)),
            dma, dma, dma, dma, dma((5 + chunks,)),
            dma((chunks,)), dma((chunks,)),
            dma((chunks, G)), dma((chunks, G)),
            dma((G,)), dma((G,)),
            dma((R // 2, 2)), dma((R,)),
        ]
        + end_scratch,
        compiler_params=pltpu.CompilerParams(
            collective_id=0, has_side_effects=True, vmem_limit_bytes=60 * 1024 * 1024
        ),
    )(hamiltonian, pattern.T, vectors, spectrum)


def solution(mesh):
    in_specs = (
        P(("kpt", "row"), "rep", None, None),
        P("row", "rep"),
        P("col", ("kpt", "row")),
        P("kpt"),
    )
    out_specs = (P("col", ("kpt", "row")), P(("kpt", "row"), "col"))
    return jax.shard_map(
        functools.partial(on_device, mesh.shape["row"], mesh.shape["col"]),
        mesh=mesh, in_specs=in_specs, out_specs=out_specs, check_vma=False,
    )
```
